32 devices in a mesh: dp: 4 (over y, x), fsdp: 4 (over z), ctx: 2 (over core).
Axes of the slice: x: 2, y: 2, z: 4, core: 2. Of those that a mesh axis runs over, the one named last changes fastest.
Arguments:
- inputs: bfloat16 [16, 1024, 768], P(('dp', 'fsdp'), 'ctx'), may hold values from -6 to 6
- cotangent: bfloat16 [16, 1024, 768], P(('dp', 'fsdp'), 'ctx'), may hold values from -6 to 6
- slot_order: int32 [4], replicated, may hold values from 0 to 3, each once
- w_qkv: bfloat16 [768, 2304], P('fsdp'), may hold values from -0.3125 to 0.3125
- w_out: bfloat16 [768, 768], P('fsdp'), may hold values from -0.875 to 0.875
- w_up: bfloat16 [768, 3072], P('fsdp'), may hold values from -0.21875 to 0.21875
- w_down: bfloat16 [3072, 768], P('fsdp'), may hold values from -0.109375 to 0.109375
- qv_bias: bfloat16 [2, 768], P(None, 'fsdp'), may hold values from -2 to 2
- out_bias: bfloat16 [768], P('fsdp'), may hold values from -2 to 2
- up_bias: bfloat16 [3072], P('fsdp'), may hold values from -3 to 3
- down_bias: bfloat16 [768], P('fsdp'), may hold values from -2 to 2
- norm1_gain: bfloat16 [768], P('fsdp'), may hold values from 0.5 to 1.5
- norm1_shift: bfloat16 [768], P('fsdp'), may hold values from -2 to 2
- norm2_gain: bfloat16 [768], P('fsdp'), may hold values from 0.5 to 1.5
- norm2_shift: bfloat16 [768], P('fsdp'), may hold values from -2 to 2
Outputs:
- outputs: bfloat16 [16, 1024, 768], P(('dp', 'fsdp'), 'ctx')
- input_grad: bfloat16 [16, 1024, 768], P(('dp', 'fsdp'), 'ctx')
- grad_w_qkv: float32 [768, 2304], P('fsdp')
- grad_w_out: float32 [768, 768], P('fsdp')
- grad_w_up: float32 [768, 3072], P('fsdp')
- grad_w_down: float32 [3072, 768], P('fsdp')
- grad_qv_bias: float32 [2, 768], P(None, 'fsdp')
- grad_out_bias: float32 [768], P('fsdp')
- grad_up_bias: float32 [3072], P('fsdp')
- grad_down_bias: float32 [768], P('fsdp')
- grad_norm1_gain: float32 [768], P('fsdp')
- grad_norm1_shift: float32 [768], P('fsdp')
- grad_norm2_gain: float32 [768], P('fsdp')
- grad_norm2_shift: float32 [768], P('fsdp')
The draws below stay inside these ranges and needn't reach their ends.
Inputs may be any that keep to these rules, and one draw needn't show every extreme that they name: Each position block number appears once; storage slot b of every sequence holds positions slot_order[b] * 256 to slot_order[b] * 256 + 255.
All inputs are finite; a program needn't handle non-finite values.
Results may differ from the reference program's by a relative error of at most 0.018.
Values may be sent and summed in bfloat16 or wider, within the bound.
A program may use at most 192 MiB of HBM per device.

```python
import jax
import jax.numpy as jnp
from jax import lax

D = 768
HEADS = 12
HD = 64
FF = 3072
SEQ = 1024
SEQS = 16
BLOCKS = 4
PIECE = 256


def level_of(key, dims, shards, low, top_value):
    def one(position, blocks):
        steps = jax.random.uniform(jax.random.fold_in(jax.random.fold_in(key, 6), position), (blocks,), jnp.float32, low / len(shards), top_value / len(shards))
        return jnp.repeat(jnp.exp(steps), dims[position] // blocks).reshape((-1,) + (1,) * (len(dims) - position - 1))

    gain = one(*shards[0])
    for cut in shards[1:]:
        gain = gain * one(*cut)
    return gain


def scatter_about(own_key, shape, deviation, most, pieces=(), kind=jnp.bfloat16):
    drawn = deviation * jax.random.normal(own_key, shape, jnp.float32)
    if pieces:
        drawn = drawn * level_of(own_key, shape, pieces, -0.22, 0.18)
    return jnp.clip(drawn, -most, most).astype(kind)


def setup_inputs(seed: int = 0) -> dict:
    key_list = jax.random.split(jax.random.key(seed), 16)
    inputs = scatter_about(key_list[0], (SEQS, SEQ, D), 1.0, 6.0, ((0, 16), (1, 2)))
    cotangent = scatter_about(key_list[1], (SEQS, SEQ, D), 1.0, 6.0, ((0, 16), (1, 2)))
    slot_order = jax.random.permutation(key_list[2], BLOCKS).astype(jnp.int32)
    w_qkv = scatter_about(key_list[3], (D, 3 * D), (D // 2) ** -0.5, 0.3125, ((0, 4),))
    w_out = scatter_about(key_list[4], (D, D), (D // 16) ** -0.5, 0.875, ((0, 4),))
    w_up = scatter_about(key_list[5], (D, FF), D ** -0.5, 0.21875, ((0, 4),))
    w_down = scatter_about(key_list[6], (FF, D), FF ** -0.5, 0.109375, ((0, 4),))
    qv_bias = scatter_about(key_list[7], (2, D), 0.3, 2.0, ((1, 4),))
    out_bias = scatter_about(key_list[8], (D,), 0.3, 2.0, ((0, 4),))
    up_bias = scatter_about(key_list[9], (FF,), 0.5, 3.0, ((0, 4),))
    down_bias = scatter_about(key_list[10], (D,), 0.3, 2.0, ((0, 4),))
    norm1_gain = jnp.clip(1.0 + 0.1 * jax.random.normal(key_list[11], (D,), jnp.float32), 0.5, 1.5).astype(jnp.bfloat16)
    norm1_shift = scatter_about(key_list[12], (D,), 0.3, 2.0, ((0, 4),))
    norm2_gain = jnp.clip(1.0 + 0.1 * jax.random.normal(key_list[13], (D,), jnp.float32), 0.5, 1.5).astype(jnp.bfloat16)
    norm2_shift = scatter_about(key_list[14], (D,), 0.3, 2.0, ((0, 4),))
    return {"inputs": inputs, "cotangent": cotangent, "slot_order": slot_order, "w_qkv": w_qkv, "w_out": w_out, "w_up": w_up, "w_down": w_down, "qv_bias": qv_bias, "out_bias": out_bias, "up_bias": up_bias, "down_bias": down_bias, "norm1_gain": norm1_gain, "norm1_shift": norm1_shift, "norm2_gain": norm2_gain, "norm2_shift": norm2_shift}


EPSILON = 1e-05
MASKED = -1e+30
GELU_COEF = 0.7978845608028654

@jax.custom_vjp
def low(v):
    return lax.optimization_barrier(v.astype(jnp.bfloat16)).astype(jnp.float32)

@jax.custom_vjp
def low_back(v):
    return v

def low_keep(v):
    return (low(v), None)

def low_pass(kept, grad):
    return (grad,)

def back_keep(v):
    return (v, None)

def back_low(kept, grad):
    return (low(grad),)
low.defvjp(low_keep, low_pass)
low_back.defvjp(back_keep, back_low)

def gelu_tanh(pre_act):
    return 0.5 * pre_act * (1.0 + jnp.tanh(GELU_COEF * (pre_act + 0.044715 * pre_act * pre_act * pre_act)))

def layer_norm(values, gain_vec, shift_vec):
    row_mean = lax.optimization_barrier(jnp.mean(values, axis=-1, keepdims=True))
    centered = values - row_mean
    variance = lax.optimization_barrier(jnp.mean(centered * centered, axis=-1, keepdims=True))
    return centered * lax.rsqrt(variance + EPSILON) * gain_vec + shift_vec

def product(left_op, right_op):
    return jnp.dot(left_op, right_op, precision=lax.Precision.HIGHEST)

def attention(queries, key_rows, values, places):
    block_rows = min(512, SEQ)
    scaling = HD ** (-0.5)
    key_heads = key_rows.reshape(SEQ, HEADS, HD)
    value_heads = values.reshape(SEQ, HEADS, HD)

    def one_block(operands):
        query_block, query_places = operands
        scores = jnp.einsum('qhd,khd->hqk', query_block, key_heads, precision=lax.Precision.HIGHEST) * scaling
        scores = low_back(scores)
        allowed = places[None, None, :] <= query_places[None, :, None]
        scores = jnp.where(allowed, scores, MASKED)
        row_max = lax.optimization_barrier(jnp.max(scores, axis=-1, keepdims=True))
        weights = jnp.where(allowed, jnp.exp(scores - row_max), 0.0)
        soft_probs = low(weights / lax.optimization_barrier(jnp.sum(weights, axis=-1, keepdims=True)))
        return jnp.einsum('hqk,khd->qhd', soft_probs, value_heads, precision=lax.Precision.HIGHEST)
    blocks = SEQ // block_rows
    results = lax.map(jax.checkpoint(one_block), (queries.reshape(blocks, block_rows, HEADS, HD), places.reshape(blocks, block_rows)))
    return results.reshape(SEQ, HEADS * HD)

def one_sequence(sequence, places, w_qkv, w_out, w_up, w_down, qv_bias, out_bias, up_bias, down_bias, norm1_gain, norm1_shift, norm2_gain, norm2_shift):
    normed = low(layer_norm(sequence, norm1_gain, norm1_shift))
    queries = low(low_back(product(normed, w_qkv[:, :D]) + qv_bias[0]))
    key_rows = low(low_back(product(normed, w_qkv[:, D:2 * D])))
    values = low(low_back(product(normed, w_qkv[:, 2 * D:]) + qv_bias[1]))
    attended = low(low_back(attention(queries, key_rows, values, places)))
    middle = sequence + low_back(product(attended, w_out) + out_bias)
    second = low(layer_norm(middle, norm2_gain, norm2_shift))
    hidden = low_back(product(second, w_up) + up_bias)
    activated = low(gelu_tanh(hidden))
    return middle + product(activated, w_down) + down_bias

def reference(inputs, cotangent, slot_order, w_qkv, w_out, w_up, w_down, qv_bias, out_bias, up_bias, down_bias, norm1_gain, norm1_shift, norm2_gain, norm2_shift):
    slot_ids = jnp.arange(SEQ, dtype=jnp.int32)
    places = (slot_order[slot_ids // PIECE] * PIECE + slot_ids % PIECE).astype(jnp.int32)
    parameters = tuple((param_array.astype(jnp.float32) for param_array in (w_qkv, w_out, w_up, w_down, qv_bias, out_bias, up_bias, down_bias, norm1_gain, norm1_shift, norm2_gain, norm2_shift)))

    def forward(sequences, *weight_list):
        return lax.map(lambda sequence: one_sequence(sequence, places, *weight_list), sequences)
    results, pull_back = jax.vjp(forward, inputs.astype(jnp.float32), *parameters)
    gradients = pull_back(cotangent.astype(jnp.float32))
    return (results.astype(jnp.bfloat16), gradients[0].astype(jnp.bfloat16), gradients[1], gradients[2], gradients[3], gradients[4], gradients[5], gradients[6], gradients[7], gradients[8], gradients[9], gradients[10], gradients[11], gradients[12])
```

```python
import math

import jax
import jax.numpy as jnp
from jax import lax
from jax.sharding import PartitionSpec as P

HEADS = 12
HD = 64


EPSILON = 1e-05
MASKED = -1e30
GELU_COEF = 0.7978845608028654


def gelu_tanh(pre_act):
    return (
        0.5
        * pre_act
        * (1.0 + jnp.tanh(GELU_COEF * (pre_act + 0.044715 * pre_act * pre_act * pre_act)))
    )


def normalize(rows_in):
    row_mean = jnp.mean(rows_in, axis=-1, keepdims=True)
    centered = rows_in - row_mean
    variance = jnp.mean(centered * centered, axis=-1, keepdims=True)
    row_scale = lax.rsqrt(variance + EPSILON)
    return (centered * row_scale, row_scale)


def norm_back(grad_out, normed, row_scale, gain_vec):
    shaped = grad_out * gain_vec
    return row_scale * (
        shaped
        - jnp.mean(shaped, axis=-1, keepdims=True)
        - normed * jnp.mean(shaped * normed, axis=-1, keepdims=True)
    )


def token_places(slot_ids, slot_order, piece_len):
    slot_block = slot_ids // piece_len
    block_ids = jnp.arange(slot_order.shape[0], dtype=jnp.int32)
    matches = (slot_block[:, None] == block_ids[None, :]).astype(jnp.int32)
    return jnp.sum(matches * slot_order[None, :], axis=1) * piece_len + slot_ids % piece_len


def attend_piece(state_now, piece_pair, queries, query_places, slot_order, piece_len, scaling):
    key_piece, value_piece = piece_pair
    seq_count = key_piece.shape[0]
    key_count = key_piece.shape[1]
    block_width = math.gcd(key_count, 512)
    block_count = key_count // block_width

    def one_block(block_index, carried):
        row_max, row_total, weighted = carried
        offset = block_index * block_width
        key_block = lax.dynamic_slice_in_dim(key_piece, offset, block_width, 1).reshape(
            seq_count, block_width, HEADS, HD
        )
        value_block = lax.dynamic_slice_in_dim(value_piece, offset, block_width, 1).reshape(
            seq_count, block_width, HEADS, HD
        )
        key_places = token_places(
            offset + jnp.arange(block_width, dtype=jnp.int32), slot_order, piece_len
        )
        scores = (
            jnp.einsum("sqhd,skhd->sqhk", queries, key_block, preferred_element_type=jnp.float32)
            * scaling
        )
        allowed = key_places[None, None, None, :] <= query_places[None, :, None, None]
        scores = jnp.where(allowed, scores, MASKED)
        new_max = jnp.maximum(row_max, jnp.max(scores, axis=-1))
        weights = jnp.where(allowed, jnp.exp(scores - new_max[..., None]), 0.0)
        factor = jnp.exp(row_max - new_max)
        row_total = row_total * factor + jnp.sum(weights, axis=-1)
        weighted = weighted * factor[..., None] + jnp.einsum(
            "sqhk,skhd->sqhd",
            weights.astype(jnp.bfloat16),
            value_block,
            preferred_element_type=jnp.float32,
        )
        return (new_max, row_total, weighted)

    return lax.fori_loop(0, block_count, one_block, state_now)


def body(
    inputs,
    cotangent,
    slot_order,
    w_qkv,
    w_out,
    w_up,
    w_down,
    qv_bias,
    out_bias,
    up_bias,
    down_bias,
    norm1_gain,
    norm1_shift,
    norm2_gain,
    norm2_shift,
):
    seq_count, local_len, model_width = inputs.shape
    row_count = seq_count * local_len
    piece_len = local_len // 2
    scaling = HD ** (-0.5)
    spread = ("fsdp", "dp", "ctx")
    copies = lax.axis_size("dp") * lax.axis_size("ctx")
    copy_index = lax.axis_index("dp") * lax.axis_size("ctx") + lax.axis_index("ctx")

    def own_piece(shard):
        rows = shard.shape[0] // copies
        return lax.dynamic_slice_in_dim(shard, copy_index * rows, rows, 0)

    def gather_whole(shard):
        return lax.all_gather(own_piece(shard), spread, axis=0, tiled=True)

    shards = lax.axis_size("fsdp")
    small_row = jnp.concatenate(
        [
            qv_bias.reshape(-1),
            out_bias,
            up_bias,
            down_bias,
            norm1_gain,
            norm1_shift,
            norm2_gain,
            norm2_shift,
        ]
    )
    small_rows = lax.all_gather(small_row, "fsdp", axis=0, tiled=False)
    part = model_width // shards

    def small_part(start, width):
        return small_rows[:, start : start + width].reshape(-1)

    whole_qv = jnp.stack([small_part(0, part), small_part(part, part)])
    whole_ob = small_part(2 * part, part)
    hidden_part = up_bias.shape[0]
    whole_ub = small_part(3 * part, hidden_part)
    rest = 3 * part + hidden_part
    whole_db = small_part(rest, part)
    gain_one = small_part(rest + part, part)
    shift_one = small_part(rest + 2 * part, part)
    gain_two = small_part(rest + 3 * part, part)
    shift_two = small_part(rest + 4 * part, part)
    whole_qkv = gather_whole(w_qkv)
    whole_out = gather_whole(w_out)
    whole_up = gather_whole(w_up)
    whole_down = gather_whole(w_down)
    flat_in = inputs.reshape(row_count, model_width).astype(jnp.float32)
    normed_one, scale_one = normalize(flat_in)
    hidden_one = (normed_one * gain_one.astype(jnp.float32) + shift_one.astype(jnp.float32)).astype(
        jnp.bfloat16
    )
    projected = jnp.dot(hidden_one, whole_qkv, preferred_element_type=jnp.float32)
    bias_rows = whole_qv.astype(jnp.float32)
    queries = (
        (projected[:, :model_width] + bias_rows[0])
        .astype(jnp.bfloat16)
        .reshape(seq_count, local_len, HEADS, HD)
    )
    key_rows = (
        projected[:, model_width : 2 * model_width]
        .astype(jnp.bfloat16)
        .reshape(seq_count, local_len, model_width)
    )
    value_rows = (
        (projected[:, 2 * model_width :] + bias_rows[1])
        .astype(jnp.bfloat16)
        .reshape(seq_count, local_len, model_width)
    )
    slot_ids = lax.axis_index("ctx") * local_len + jnp.arange(local_len, dtype=jnp.int32)
    query_places = token_places(slot_ids, slot_order, piece_len)
    start_state = (
        jnp.full((seq_count, local_len, HEADS), MASKED, jnp.float32),
        jnp.zeros((seq_count, local_len, HEADS), jnp.float32),
        jnp.zeros((seq_count, local_len, HEADS, HD), jnp.float32),
    )
    final_state = attend_piece(
        start_state,
        (
            lax.all_gather(key_rows, "ctx", axis=1, tiled=True),
            lax.all_gather(value_rows, "ctx", axis=1, tiled=True),
        ),
        queries,
        query_places,
        slot_order,
        piece_len,
        scaling,
    )
    row_max, row_total, weighted = final_state
    attended_f32 = weighted / row_total[..., None]
    log_total = row_max + jnp.log(row_total)
    attended = attended_f32.reshape(row_count, model_width).astype(jnp.bfloat16)
    middle = (
        flat_in
        + jnp.dot(attended, whole_out, preferred_element_type=jnp.float32)
        + whole_ob.astype(jnp.float32)
    )
    normed_two, scale_two = normalize(middle)
    hidden_two = (normed_two * gain_two.astype(jnp.float32) + shift_two.astype(jnp.float32)).astype(
        jnp.bfloat16
    )
    pre_act = jnp.dot(hidden_two, whole_up, preferred_element_type=jnp.float32) + whole_ub.astype(
        jnp.float32
    )
    activated = gelu_tanh(pre_act).astype(jnp.bfloat16)
    result = (
        middle
        + jnp.dot(activated, whole_down, preferred_element_type=jnp.float32)
        + whole_db.astype(jnp.float32)
    )
    outputs = result.astype(jnp.bfloat16).reshape(seq_count, local_len, model_width)
    grad_rows = cotangent.reshape(row_count, model_width)
    grad_rows_f32 = grad_rows.astype(jnp.float32)
    grad_down = jnp.einsum("rf,rd->fd", activated, grad_rows, preferred_element_type=jnp.float32)
    grad_down_bias = jnp.sum(grad_rows_f32, axis=0)
    grad_act = jnp.einsum("rd,fd->rf", grad_rows, whole_down, preferred_element_type=jnp.float32)
    gelu_value, gelu_pull = jax.vjp(gelu_tanh, pre_act)
    grad_pre = gelu_pull(grad_act)[0].astype(jnp.bfloat16)
    grad_up = jnp.einsum("rd,rf->df", hidden_two, grad_pre, preferred_element_type=jnp.float32)
    grad_up_bias = jnp.sum(grad_pre.astype(jnp.float32), axis=0)
    grad_hidden_two = jnp.einsum(
        "rf,df->rd", grad_pre, whole_up, preferred_element_type=jnp.float32
    )
    grad_gain_two = jnp.sum(grad_hidden_two * normed_two, axis=0)
    grad_shift_two = jnp.sum(grad_hidden_two, axis=0)
    grad_middle = grad_rows_f32 + norm_back(
        grad_hidden_two, normed_two, scale_two, gain_two.astype(jnp.float32)
    )
    grad_branch = grad_middle.astype(jnp.bfloat16)
    grad_out = jnp.einsum("rd,re->de", attended, grad_branch, preferred_element_type=jnp.float32)
    grad_out_bias = jnp.sum(grad_branch.astype(jnp.float32), axis=0)
    grad_attended = (
        jnp.einsum("re,de->rd", grad_branch, whole_out, preferred_element_type=jnp.float32)
        .astype(jnp.bfloat16)
        .reshape(seq_count, local_len, HEADS, HD)
    )
    row_delta = jnp.sum(grad_attended.astype(jnp.float32) * attended_f32, axis=-1)
    gathered = (
        lax.all_gather(key_rows, "ctx", axis=1, tiled=True),
        lax.all_gather(value_rows, "ctx", axis=1, tiled=True),
    )
    gathered_keys, gathered_values = gathered
    key_count = gathered_keys.shape[1]
    block_width = math.gcd(local_len, 512)
    block_count = key_count // block_width

    def score_grads(
        query_block,
        grad_block,
        total_block,
        delta_block,
        block_places,
        key_block,
        value_block,
        key_places,
    ):
        allowed = key_places[None, None, None, :] <= block_places[None, :, None, None]
        scores = (
            jnp.einsum(
                "sqhd,skhd->sqhk", query_block, key_block, preferred_element_type=jnp.float32
            )
            * scaling
        )
        soft_probs = jnp.where(
            allowed, jnp.exp(jnp.where(allowed, scores - total_block[..., None], 0.0)), 0.0
        )
        grad_probs = jnp.einsum(
            "sqhd,skhd->sqhk", grad_block, value_block, preferred_element_type=jnp.float32
        )
        grad_scores = (soft_probs * (grad_probs - delta_block[..., None])).astype(jnp.bfloat16)
        return (soft_probs, grad_scores)

    def remote_block(offset):
        key_block = lax.dynamic_slice_in_dim(gathered_keys, offset, block_width, 1).reshape(
            seq_count, block_width, HEADS, HD
        )
        value_block = lax.dynamic_slice_in_dim(gathered_values, offset, block_width, 1).reshape(
            seq_count, block_width, HEADS, HD
        )
        key_places = token_places(
            offset + jnp.arange(block_width, dtype=jnp.int32), slot_order, piece_len
        )
        soft_probs, grad_scores = score_grads(
            queries,
            grad_attended,
            log_total,
            row_delta,
            query_places,
            key_block,
            value_block,
            key_places,
        )
        return (key_block, soft_probs, grad_scores)

    zero_queries = jnp.zeros((seq_count, local_len, HEADS, HD), jnp.float32)

    def back_block(grad_queries, block_index):
        key_block, soft_probs, grad_scores = remote_block(block_index * block_width)
        grad_queries = (
            grad_queries
            + jnp.einsum(
                "sqhk,skhd->sqhd", grad_scores, key_block, preferred_element_type=jnp.float32
            )
            * scaling
        )
        grad_keys = (
            jnp.einsum("sqhk,sqhd->skhd", grad_scores, queries, preferred_element_type=jnp.float32)
            * scaling
        )
        grad_values = jnp.einsum(
            "sqhk,sqhd->skhd",
            soft_probs.astype(jnp.bfloat16),
            grad_attended,
            preferred_element_type=jnp.float32,
        )
        key_term = jnp.concatenate(
            [
                grad_keys.reshape(seq_count, block_width, model_width),
                grad_values.reshape(seq_count, block_width, model_width),
            ],
            axis=-1,
        )
        return (grad_queries, key_term)

    grad_queries, key_terms = lax.scan(
        back_block, zero_queries, jnp.arange(block_count, dtype=jnp.int32)
    )
    own_terms = lax.psum_scatter(
        key_terms.astype(jnp.bfloat16), "ctx", scatter_dimension=0, tiled=True
    ).astype(jnp.float32)
    own_terms = own_terms.transpose(1, 0, 2, 3).reshape(row_count, 2 * model_width)
    grad_qkv = jnp.concatenate(
        [grad_queries.reshape(row_count, model_width), own_terms], axis=-1
    ).astype(jnp.bfloat16)
    grad_qkv_w = jnp.einsum("rd,re->de", hidden_one, grad_qkv, preferred_element_type=jnp.float32)
    column_sums = jnp.sum(grad_qkv.astype(jnp.float32), axis=0)
    grad_qv_bias = jnp.stack([column_sums[:model_width], column_sums[2 * model_width :]])
    grad_hidden_one = jnp.einsum(
        "re,de->rd", grad_qkv, whole_qkv, preferred_element_type=jnp.float32
    )
    grad_gain_one = jnp.sum(grad_hidden_one * normed_one, axis=0)
    grad_shift_one = jnp.sum(grad_hidden_one, axis=0)
    grad_inputs = (
        (
            grad_middle
            + norm_back(grad_hidden_one, normed_one, scale_one, gain_one.astype(jnp.float32))
        )
        .astype(jnp.bfloat16)
        .reshape(seq_count, local_len, model_width)
    )
    def share(grad):
        piece = lax.psum_scatter(
            grad.astype(jnp.bfloat16), spread, scatter_dimension=0, tiled=True
        )
        return lax.all_gather(piece, ("dp", "ctx"), axis=0, tiled=True).astype(jnp.float32)

    small_grads = jnp.concatenate(
        [
            grad_qv_bias[0].reshape(shards, part),
            grad_qv_bias[1].reshape(shards, part),
            grad_out_bias.reshape(shards, part),
            grad_up_bias.reshape(shards, hidden_part),
            grad_down_bias.reshape(shards, part),
            grad_gain_one.reshape(shards, part),
            grad_shift_one.reshape(shards, part),
            grad_gain_two.reshape(shards, part),
            grad_shift_two.reshape(shards, part),
        ],
        axis=1,
    )
    small_width = small_grads.shape[1]
    piece_width = small_width // copies
    out_rows = model_width // (shards * copies)
    packed = jnp.concatenate(
        [
            grad_out.astype(jnp.bfloat16).reshape(shards * copies, out_rows, model_width),
            jnp.pad(
                small_grads.astype(jnp.bfloat16).reshape(shards * copies, 1, piece_width),
                ((0, 0), (0, 7), (0, model_width - piece_width)),
            ),
        ],
        axis=1,
    )
    own_down = share(grad_down)
    own_up = share(grad_up)
    own_qkv = share(grad_qkv_w)
    own_packed = share(packed)
    own_out = own_packed[:, :out_rows].reshape(copies * out_rows, model_width)
    own_small = own_packed[:, out_rows, :piece_width].reshape(small_width)

    def own_part(start, width):
        return own_small[start : start + width]

    return (
        outputs,
        grad_inputs,
        own_qkv,
        own_out,
        own_up,
        own_down,
        own_part(0, 2 * part).reshape(2, part),
        own_part(2 * part, part),
        own_part(3 * part, hidden_part),
        own_part(rest, part),
        own_part(rest + part, part),
        own_part(rest + 2 * part, part),
        own_part(rest + 3 * part, part),
        own_part(rest + 4 * part, part),
    )


def solution(mesh):
    return jax.shard_map(
        body,
        mesh=mesh,
        in_specs=(
            P(("dp", "fsdp"), "ctx", None),
            P(("dp", "fsdp"), "ctx", None),
            P(),
            P("fsdp", None),
            P("fsdp", None),
            P("fsdp", None),
            P("fsdp", None),
            P(None, "fsdp"),
            P("fsdp"),
            P("fsdp"),
            P("fsdp"),
            P("fsdp"),
            P("fsdp"),
            P("fsdp"),
            P("fsdp"),
        ),
        out_specs=(
            P(("dp", "fsdp"), "ctx", None),
            P(("dp", "fsdp"), "ctx", None),
            P("fsdp", None),
            P("fsdp", None),
            P("fsdp", None),
            P("fsdp", None),
            P(None, "fsdp"),
            P("fsdp"),
            P("fsdp"),
            P("fsdp"),
            P("fsdp"),
            P("fsdp"),
            P("fsdp"),
            P("fsdp"),
        ),
        check_vma=False,
    )
```

```python
import math

import jax
import jax.numpy as jnp
from jax import lax
from jax.experimental import pallas as pl
from jax.experimental.pallas import tpu as pltpu
from jax.sharding import PartitionSpec as P

HEADS = 12
HD = 64


EPSILON = 1e-05
MASKED = -1e30
GELU_COEF = 0.7978845608028654


def gelu_tanh(pre_act):
    return (
        0.5
        * pre_act
        * (1.0 + jnp.tanh(GELU_COEF * (pre_act + 0.044715 * pre_act * pre_act * pre_act)))
    )


def normalize(rows_in):
    row_mean = jnp.mean(rows_in, axis=-1, keepdims=True)
    centered = rows_in - row_mean
    variance = jnp.mean(centered * centered, axis=-1, keepdims=True)
    row_scale = lax.rsqrt(variance + EPSILON)
    return (centered * row_scale, row_scale)


def norm_back(grad_out, normed, row_scale, gain_vec):
    shaped = grad_out * gain_vec
    return row_scale * (
        shaped
        - jnp.mean(shaped, axis=-1, keepdims=True)
        - normed * jnp.mean(shaped * normed, axis=-1, keepdims=True)
    )


def token_places(slot_ids, slot_order, piece_len):
    slot_block = slot_ids // piece_len
    block_ids = jnp.arange(slot_order.shape[0], dtype=jnp.int32)
    matches = (slot_block[:, None] == block_ids[None, :]).astype(jnp.int32)
    return jnp.sum(matches * slot_order[None, :], axis=1) * piece_len + slot_ids % piece_len


def attend_piece(state_now, piece_pair, queries, query_places, slot_order, piece_len, scaling):
    key_piece, value_piece = piece_pair
    seq_count = key_piece.shape[0]
    key_count = key_piece.shape[1]
    block_width = math.gcd(key_count, 512)
    block_count = key_count // block_width

    def one_block(block_index, carried):
        row_max, row_total, weighted = carried
        offset = block_index * block_width
        key_block = lax.dynamic_slice_in_dim(key_piece, offset, block_width, 1).reshape(
            seq_count, block_width, HEADS, HD
        )
        value_block = lax.dynamic_slice_in_dim(value_piece, offset, block_width, 1).reshape(
            seq_count, block_width, HEADS, HD
        )
        key_places = token_places(
            offset + jnp.arange(block_width, dtype=jnp.int32), slot_order, piece_len
        )
        scores = (
            jnp.einsum("sqhd,skhd->sqhk", queries, key_block, preferred_element_type=jnp.float32)
            * scaling
        )
        allowed = key_places[None, None, None, :] <= query_places[None, :, None, None]
        scores = jnp.where(allowed, scores, MASKED)
        new_max = jnp.maximum(row_max, jnp.max(scores, axis=-1))
        weights = jnp.where(allowed, jnp.exp(scores - new_max[..., None]), 0.0)
        factor = jnp.exp(row_max - new_max)
        row_total = row_total * factor + jnp.sum(weights, axis=-1)
        weighted = weighted * factor[..., None] + jnp.einsum(
            "sqhk,skhd->sqhd",
            weights.astype(jnp.bfloat16),
            value_block,
            preferred_element_type=jnp.float32,
        )
        return (new_max, row_total, weighted)

    return lax.fori_loop(0, block_count, one_block, state_now)


TILE = 16
MESH_ID = pl.DeviceIdType.MESH


def peer_table():
    dp, z, core = lax.axis_index("dp"), lax.axis_index("fsdp"), lax.axis_index("ctx")
    row, col = dp // 2, dp % 2
    sibling = {"ctx": 1 - core}
    beside = {"dp": row * 2 + (1 - col)}
    above = {"dp": (1 - row) * 2 + col}
    across = {"dp": (1 - row) * 2 + (1 - col)}
    return row, col, z, core, sibling, beside, above, across


def greet(peers):
    barrier = pltpu.get_barrier_semaphore()
    for peer in peers:
        pl.semaphore_signal(barrier, inc=1, device_id=peer, device_id_type=MESH_ID)
    pl.semaphore_wait(barrier, len(peers))


def push(source, target, sems, slot, peer):
    return pltpu.make_async_remote_copy(
        src_ref=source,
        dst_ref=target,
        send_sem=sems.at[0, slot],
        recv_sem=sems.at[1, slot],
        device_id=peer,
        device_id_type=MESH_ID,
    )


def gather_kernel(own, whole, line_sems, plane_sems, pair_sems, local_sem):
    row, col, z, core, sibling, beside, above, across = peer_table()
    line_peers = [{"fsdp": lax.rem(z + 4 - k, 4)} for k in (1, 2, 3)]
    greet([sibling, beside, above, across] + line_peers)
    keep = pltpu.make_async_copy(own, whole.at[z], local_sem)
    keep.start()
    line = [
        push(own.at[core, row, col], whole.at[z, core, row, col], line_sems, k, line_peers[k])
        for k in (0, 2, 1)
    ]
    for copy in line:
        copy.start()
    plane = []
    origins = [lax.rem(z + 1 + k, 4) for k in (0, 2, 1)]
    for step, origin in enumerate(origins):
        line[step].wait_recv()
        piece = whole.at[origin, core, row, col]
        plane.append(
            [
                push(piece, piece, plane_sems, step * 3 + index, peer)
                for index, peer in enumerate((beside, above, across))
            ]
        )
        for copy in plane[-1]:
            copy.start()
    pair = []
    for step, origin in enumerate(origins):
        for copy in plane[step]:
            copy.wait_recv()
        half = whole.at[origin, core]
        pair.append(push(half, half, pair_sems, step, sibling))
        pair[-1].start()
    for copy in pair:
        copy.wait()
    for copies in plane:
        for copy in copies:
            copy.wait_send()
    for copy in line:
        copy.wait_send()
    keep.wait()


def gather_bundle(own):
    rows, width = own.shape[-2:]
    return pl.pallas_call(
        gather_kernel,
        out_shape=jax.ShapeDtypeStruct((4, 2, 2, 2, rows, width), own.dtype),
        in_specs=[pl.BlockSpec(memory_space=pl.ANY)],
        out_specs=pl.BlockSpec(memory_space=pl.ANY),
        scratch_shapes=[
            pltpu.SemaphoreType.DMA((2, 3)),
            pltpu.SemaphoreType.DMA((2, 9)),
            pltpu.SemaphoreType.DMA((2, 3)),
            pltpu.SemaphoreType.DMA,
        ],
        compiler_params=pltpu.CompilerParams(collective_id=1, has_side_effects=True),
        name="gather_weights",
    )(own)


def add_rows(target, target_at, source, source_at, start, count, source_start):
    @pl.loop(0, count // TILE)
    def _(step):
        offset = pl.multiple_of(step * TILE, TILE)
        here = target_at + (pl.ds(start + offset, TILE),)
        there = source_at + (pl.ds(source_start + offset, TILE),)
        target[here] = (
            target[here].astype(jnp.float32) + source[there].astype(jnp.float32)
        ).astype(target.dtype)


def sum_kernel(
    grads,
    shared,
    held,
    from_pair,
    from_beside,
    from_above,
    late_beside,
    late_above,
    from_line,
    done,
    load_sems,
    pair_sems,
    beside_sems,
    above_sems,
    late_beside_sems,
    late_above_sems,
    line_sems,
    plane_sems,
    last_sems,
    local_sem,
):
    row, col, z, core, sibling, beside, above, across = peer_table()
    rows = grads.shape[-2]
    cut = (rows // 2 + TILE - 1) // TILE * TILE
    tail = rows - cut
    order = [lax.rem(z + 1 + k, 4) for k in range(4)]
    line_peers = [{"fsdp": order[k]} for k in range(3)]
    greet([sibling, beside, above, across] + line_peers)
    loads, pairs = [], []
    for k in range(4):
        pairs.append(push(grads.at[order[k], 1 - core], from_pair.at[k], pair_sems, k, sibling))
        pairs[-1].start()
        loads.append(pltpu.make_async_copy(grads.at[order[k], core], held.at[k], load_sems.at[k]))
        loads[-1].start()
    first = []
    for k in range(4):
        loads[k].wait()
        pairs[k].wait_recv()
        for r in range(2):
            for c in range(2):
                add_rows(held, (k, r, c), from_pair, (k, r, c), 0, rows, 0)
        first.append(
            (
                push(
                    held.at[k, :, 1 - col, pl.ds(0, cut)],
                    from_beside.at[k],
                    beside_sems,
                    k,
                    beside,
                ),
                push(
                    held.at[k, 1 - row, :, pl.ds(cut, tail)],
                    from_above.at[k],
                    above_sems,
                    k,
                    above,
                ),
            )
        )
        for copy in first[-1]:
            copy.start()
    second = []
    for k in range(4):
        for copy in first[k]:
            copy.wait_recv()
        for other in range(2):
            add_rows(held, (k, other, col), from_beside, (k, other), 0, cut, 0)
            add_rows(held, (k, row, other), from_above, (k, other), cut, tail, 0)
        second.append(
            (
                push(
                    held.at[k, 1 - row, col, pl.ds(0, cut)],
                    late_above.at[k],
                    late_above_sems,
                    k,
                    above,
                ),
                push(
                    held.at[k, row, 1 - col, pl.ds(cut, tail)],
                    late_beside.at[k],
                    late_beside_sems,
                    k,
                    beside,
                ),
            )
        )
        for copy in second[-1]:
            copy.start()
    line = []
    for k in range(4):
        for copy in second[k]:
            copy.wait_recv()
        add_rows(held, (k, row, col), late_above, (k,), 0, cut, 0)
        add_rows(held, (k, row, col), late_beside, (k,), cut, tail, 0)
        if k < 3:
            line.append(push(held.at[k, row, col], from_line.at[k], line_sems, k, line_peers[k]))
            line[-1].start()
    for copy in line:
        copy.wait_recv()

    @pl.loop(0, rows // TILE)
    def _(step):
        here = pl.ds(pl.multiple_of(step * TILE, TILE), TILE)
        total = held[3, row, col, here].astype(jnp.float32)
        for k in range(3):
            total = total + from_line[k, here].astype(jnp.float32)
        done[core, row, col, here] = total.astype(done.dtype)

    piece = done.at[core, row, col]
    plane = [
        push(piece, piece, plane_sems, index, peer)
        for index, peer in enumerate((beside, above, across))
    ]
    for copy in plane:
        copy.start()
    for copy in plane:
        copy.wait_recv()
    last = push(done.at[core], done.at[core], last_sems, 0, sibling)
    last.start()
    for copies in first + second:
        for copy in copies:
            copy.wait_send()
    for copy in pairs + line + plane:
        copy.wait_send()
    last.wait()
    out = pltpu.make_async_copy(done, shared, local_sem)
    out.start()
    out.wait()


def sum_bundle(grads):
    rows, width = grads.shape[-2:]
    kind = grads.dtype
    cut = (rows // 2 + TILE - 1) // TILE * TILE
    tail = rows - cut
    return pl.pallas_call(
        sum_kernel,
        out_shape=jax.ShapeDtypeStruct((2, 2, 2, rows, width), kind),
        in_specs=[pl.BlockSpec(memory_space=pl.ANY)],
        out_specs=pl.BlockSpec(memory_space=pl.ANY),
        scratch_shapes=[
            pltpu.VMEM((4, 2, 2, rows, width), kind),
            pltpu.VMEM((4, 2, 2, rows, width), kind),
            pltpu.VMEM((4, 2, cut, width), kind),
            pltpu.VMEM((4, 2, tail, width), kind),
            pltpu.VMEM((4, tail, width), kind),
            pltpu.VMEM((4, cut, width), kind),
            pltpu.VMEM((3, rows, width), kind),
            pltpu.VMEM((2, 2, 2, rows, width), kind),
            pltpu.SemaphoreType.DMA((4,)),
            pltpu.SemaphoreType.DMA((2, 4)),
            pltpu.SemaphoreType.DMA((2, 4)),
            pltpu.SemaphoreType.DMA((2, 4)),
            pltpu.SemaphoreType.DMA((2, 4)),
            pltpu.SemaphoreType.DMA((2, 4)),
            pltpu.SemaphoreType.DMA((2, 3)),
            pltpu.SemaphoreType.DMA((2, 3)),
            pltpu.SemaphoreType.DMA((2, 1)),
            pltpu.SemaphoreType.DMA,
        ],
        compiler_params=pltpu.CompilerParams(
            collective_id=2, has_side_effects=True, vmem_limit_bytes=48 * 1024 * 1024
        ),
        name="sum_gradients",
    )(grads)


def body(
    inputs,
    cotangent,
    slot_order,
    w_qkv,
    w_out,
    w_up,
    w_down,
    qv_bias,
    out_bias,
    up_bias,
    down_bias,
    norm1_gain,
    norm1_shift,
    norm2_gain,
    norm2_shift,
):
    seq_count, local_len, model_width = inputs.shape
    row_count = seq_count * local_len
    piece_len = local_len // 2
    scaling = HD ** (-0.5)
    spread = ("fsdp", "dp", "ctx")
    copies = lax.axis_size("dp") * lax.axis_size("ctx")
    copy_index = lax.axis_index("dp") * lax.axis_size("ctx") + lax.axis_index("ctx")

    def own_piece(shard):
        rows = shard.shape[0] // copies
        return lax.dynamic_slice_in_dim(shard, copy_index * rows, rows, 0)

    def gather_whole(shard):
        return lax.all_gather(own_piece(shard), spread, axis=0, tiled=True)

    shards = lax.axis_size("fsdp")
    small_row = jnp.concatenate(
        [
            qv_bias.reshape(-1),
            out_bias,
            up_bias,
            down_bias,
            norm1_gain,
            norm1_shift,
            norm2_gain,
            norm2_shift,
        ]
    )
    part = model_width // shards
    fits = (lax.axis_size("dp"), shards, lax.axis_size("ctx")) == (4, 4, 2)
    widths = [w_qkv.shape[1], w_out.shape[1], w_up.shape[1], w_down.shape[1]]
    depths = [w.shape[0] // copies for w in (w_qkv, w_out, w_up, w_down)]
    small_lines = small_row.shape[0] // model_width
    spare = -small_lines % TILE

    def stack_rows(matrices, small):
        groups = small.shape[0]
        parts = [
            m.reshape(groups, copies, rows, width // model_width, model_width)
            .swapaxes(2, 3)
            .reshape(groups, copies, -1, model_width)
            for m, rows, width in zip(matrices, depths, widths)
        ]
        lines = small.reshape(groups, 1, small_lines, model_width)
        parts.append(jnp.pad(lines, ((0, 0), (0, copies - 1), (0, spare), (0, 0))))
        return jnp.concatenate(parts, axis=2).reshape(groups, 2, 2, 2, -1, model_width)

    def unstack_rows(bundle):
        groups = bundle.shape[0]
        bundle = bundle.reshape(groups, copies, -1, model_width)
        found, start = [], 0
        for rows, width in zip(depths, widths):
            blocks = []
            for _ in range(width // model_width):
                blocks.append(bundle[:, :, start : start + rows].reshape(-1, model_width))
                start += rows
            found.append(blocks)
        small = bundle[:, 0, start : start + small_lines].reshape(groups, -1)
        return found, small

    if fits:
        (qkv_blocks, out_blocks, up_blocks, down_blocks), small_rows = unstack_rows(
            gather_bundle(stack_rows((w_qkv, w_out, w_up, w_down), small_row[None])[0])
        )
        whole_qkv = jnp.concatenate(qkv_blocks, axis=1)
        whole_out = out_blocks[0]
        whole_up = jnp.concatenate(up_blocks, axis=1)
        whole_down = down_blocks[0]
    else:
        small_rows = lax.all_gather(small_row, "fsdp", axis=0, tiled=False)
        whole_qkv = gather_whole(w_qkv)
        whole_out = gather_whole(w_out)
        whole_up = gather_whole(w_up)
        whole_down = gather_whole(w_down)

    def small_part(start, width):
        return small_rows[:, start : start + width].reshape(-1)

    whole_qv = jnp.stack([small_part(0, part), small_part(part, part)])
    whole_ob = small_part(2 * part, part)
    hidden_part = up_bias.shape[0]
    whole_ub = small_part(3 * part, hidden_part)
    rest = 3 * part + hidden_part
    whole_db = small_part(rest, part)
    gain_one = small_part(rest + part, part)
    shift_one = small_part(rest + 2 * part, part)
    gain_two = small_part(rest + 3 * part, part)
    shift_two = small_part(rest + 4 * part, part)
    flat_in = inputs.reshape(row_count, model_width).astype(jnp.float32)
    normed_one, scale_one = normalize(flat_in)
    hidden_one = (normed_one * gain_one.astype(jnp.float32) + shift_one.astype(jnp.float32)).astype(
        jnp.bfloat16
    )
    projected = jnp.dot(hidden_one, whole_qkv, preferred_element_type=jnp.float32)
    bias_rows = whole_qv.astype(jnp.float32)
    queries = (
        (projected[:, :model_width] + bias_rows[0])
        .astype(jnp.bfloat16)
        .reshape(seq_count, local_len, HEADS, HD)
    )
    key_rows = (
        projected[:, model_width : 2 * model_width]
        .astype(jnp.bfloat16)
        .reshape(seq_count, local_len, model_width)
    )
    value_rows = (
        (projected[:, 2 * model_width :] + bias_rows[1])
        .astype(jnp.bfloat16)
        .reshape(seq_count, local_len, model_width)
    )
    slot_ids = lax.axis_index("ctx") * local_len + jnp.arange(local_len, dtype=jnp.int32)
    query_places = token_places(slot_ids, slot_order, piece_len)
    start_state = (
        jnp.full((seq_count, local_len, HEADS), MASKED, jnp.float32),
        jnp.zeros((seq_count, local_len, HEADS), jnp.float32),
        jnp.zeros((seq_count, local_len, HEADS, HD), jnp.float32),
    )
    final_state = attend_piece(
        start_state,
        (
            lax.all_gather(key_rows, "ctx", axis=1, tiled=True),
            lax.all_gather(value_rows, "ctx", axis=1, tiled=True),
        ),
        queries,
        query_places,
        slot_order,
        piece_len,
        scaling,
    )
    row_max, row_total, weighted = final_state
    attended_f32 = weighted / row_total[..., None]
    log_total = row_max + jnp.log(row_total)
    attended = attended_f32.reshape(row_count, model_width).astype(jnp.bfloat16)
    middle = (
        flat_in
        + jnp.dot(attended, whole_out, preferred_element_type=jnp.float32)
        + whole_ob.astype(jnp.float32)
    )
    normed_two, scale_two = normalize(middle)
    hidden_two = (normed_two * gain_two.astype(jnp.float32) + shift_two.astype(jnp.float32)).astype(
        jnp.bfloat16
    )
    pre_act = jnp.dot(hidden_two, whole_up, preferred_element_type=jnp.float32) + whole_ub.astype(
        jnp.float32
    )
    activated = gelu_tanh(pre_act).astype(jnp.bfloat16)
    result = (
        middle
        + jnp.dot(activated, whole_down, preferred_element_type=jnp.float32)
        + whole_db.astype(jnp.float32)
    )
    outputs = result.astype(jnp.bfloat16).reshape(seq_count, local_len, model_width)
    grad_rows = cotangent.reshape(row_count, model_width)
    grad_rows_f32 = grad_rows.astype(jnp.float32)
    grad_down = jnp.einsum("rf,rd->fd", activated, grad_rows, preferred_element_type=jnp.float32)
    grad_down_bias = jnp.sum(grad_rows_f32, axis=0)
    grad_act = jnp.einsum("rd,fd->rf", grad_rows, whole_down, preferred_element_type=jnp.float32)
    gelu_value, gelu_pull = jax.vjp(gelu_tanh, pre_act)
    grad_pre = gelu_pull(grad_act)[0].astype(jnp.bfloat16)
    grad_up = jnp.einsum("rd,rf->df", hidden_two, grad_pre, preferred_element_type=jnp.float32)
    grad_up_bias = jnp.sum(grad_pre.astype(jnp.float32), axis=0)
    grad_hidden_two = jnp.einsum(
        "rf,df->rd", grad_pre, whole_up, preferred_element_type=jnp.float32
    )
    grad_gain_two = jnp.sum(grad_hidden_two * normed_two, axis=0)
    grad_shift_two = jnp.sum(grad_hidden_two, axis=0)
    grad_middle = grad_rows_f32 + norm_back(
        grad_hidden_two, normed_two, scale_two, gain_two.astype(jnp.float32)
    )
    grad_branch = grad_middle.astype(jnp.bfloat16)
    grad_out = jnp.einsum("rd,re->de", attended, grad_branch, preferred_element_type=jnp.float32)
    grad_out_bias = jnp.sum(grad_branch.astype(jnp.float32), axis=0)
    grad_attended = (
        jnp.einsum("re,de->rd", grad_branch, whole_out, preferred_element_type=jnp.float32)
        .astype(jnp.bfloat16)
        .reshape(seq_count, local_len, HEADS, HD)
    )
    row_delta = jnp.sum(grad_attended.astype(jnp.float32) * attended_f32, axis=-1)
    gathered = (
        lax.all_gather(key_rows, "ctx", axis=1, tiled=True),
        lax.all_gather(value_rows, "ctx", axis=1, tiled=True),
    )
    gathered_keys, gathered_values = gathered
    key_count = gathered_keys.shape[1]
    block_width = math.gcd(local_len, 512)
    block_count = key_count // block_width

    def score_grads(
        query_block,
        grad_block,
        total_block,
        delta_block,
        block_places,
        key_block,
        value_block,
        key_places,
    ):
        allowed = key_places[None, None, None, :] <= block_places[None, :, None, None]
        scores = (
            jnp.einsum(
                "sqhd,skhd->sqhk", query_block, key_block, preferred_element_type=jnp.float32
            )
            * scaling
        )
        soft_probs = jnp.where(
            allowed, jnp.exp(jnp.where(allowed, scores - total_block[..., None], 0.0)), 0.0
        )
        grad_probs = jnp.einsum(
            "sqhd,skhd->sqhk", grad_block, value_block, preferred_element_type=jnp.float32
        )
        grad_scores = (soft_probs * (grad_probs - delta_block[..., None])).astype(jnp.bfloat16)
        return (soft_probs, grad_scores)

    def remote_block(offset):
        key_block = lax.dynamic_slice_in_dim(gathered_keys, offset, block_width, 1).reshape(
            seq_count, block_width, HEADS, HD
        )
        value_block = lax.dynamic_slice_in_dim(gathered_values, offset, block_width, 1).reshape(
            seq_count, block_width, HEADS, HD
        )
        key_places = token_places(
            offset + jnp.arange(block_width, dtype=jnp.int32), slot_order, piece_len
        )
        soft_probs, grad_scores = score_grads(
            queries,
            grad_attended,
            log_total,
            row_delta,
            query_places,
            key_block,
            value_block,
            key_places,
        )
        return (key_block, soft_probs, grad_scores)

    zero_queries = jnp.zeros((seq_count, local_len, HEADS, HD), jnp.float32)

    def back_block(grad_queries, block_index):
        key_block, soft_probs, grad_scores = remote_block(block_index * block_width)
        grad_queries = (
            grad_queries
            + jnp.einsum(
                "sqhk,skhd->sqhd", grad_scores, key_block, preferred_element_type=jnp.float32
            )
            * scaling
        )
        grad_keys = (
            jnp.einsum("sqhk,sqhd->skhd", grad_scores, queries, preferred_element_type=jnp.float32)
            * scaling
        )
        grad_values = jnp.einsum(
            "sqhk,sqhd->skhd",
            soft_probs.astype(jnp.bfloat16),
            grad_attended,
            preferred_element_type=jnp.float32,
        )
        key_term = jnp.concatenate(
            [
                grad_keys.reshape(seq_count, block_width, model_width),
                grad_values.reshape(seq_count, block_width, model_width),
            ],
            axis=-1,
        )
        return (grad_queries, key_term)

    grad_queries, key_terms = lax.scan(
        back_block, zero_queries, jnp.arange(block_count, dtype=jnp.int32)
    )
    own_terms = lax.psum_scatter(
        key_terms.astype(jnp.bfloat16), "ctx", scatter_dimension=0, tiled=True
    ).astype(jnp.float32)
    own_terms = own_terms.transpose(1, 0, 2, 3).reshape(row_count, 2 * model_width)
    grad_qkv = jnp.concatenate(
        [grad_queries.reshape(row_count, model_width), own_terms], axis=-1
    ).astype(jnp.bfloat16)
    grad_qkv_w = jnp.einsum("rd,re->de", hidden_one, grad_qkv, preferred_element_type=jnp.float32)
    column_sums = jnp.sum(grad_qkv.astype(jnp.float32), axis=0)
    grad_qv_bias = jnp.stack([column_sums[:model_width], column_sums[2 * model_width :]])
    grad_hidden_one = jnp.einsum(
        "re,de->rd", grad_qkv, whole_qkv, preferred_element_type=jnp.float32
    )
    grad_gain_one = jnp.sum(grad_hidden_one * normed_one, axis=0)
    grad_shift_one = jnp.sum(grad_hidden_one, axis=0)
    grad_inputs = (
        (
            grad_middle
            + norm_back(grad_hidden_one, normed_one, scale_one, gain_one.astype(jnp.float32))
        )
        .astype(jnp.bfloat16)
        .reshape(seq_count, local_len, model_width)
    )
    def share(grad):
        piece = lax.psum_scatter(
            grad.astype(jnp.bfloat16), spread, scatter_dimension=0, tiled=True
        )
        return lax.all_gather(piece, ("dp", "ctx"), axis=0, tiled=True).astype(jnp.float32)

    small_grads = jnp.concatenate(
        [
            grad_qv_bias[0].reshape(shards, part),
            grad_qv_bias[1].reshape(shards, part),
            grad_out_bias.reshape(shards, part),
            grad_up_bias.reshape(shards, hidden_part),
            grad_down_bias.reshape(shards, part),
            grad_gain_one.reshape(shards, part),
            grad_shift_one.reshape(shards, part),
            grad_gain_two.reshape(shards, part),
            grad_shift_two.reshape(shards, part),
        ],
        axis=1,
    )
    small_width = small_grads.shape[1]
    if fits:
        grads = [g.astype(jnp.bfloat16) for g in (grad_qkv_w, grad_out, grad_up, grad_down)]
        found, own_small = unstack_rows(
            sum_bundle(stack_rows(grads, small_grads.astype(jnp.bfloat16)))[None]
        )
        own_qkv, own_out, own_up, own_down = (
            jnp.concatenate([block.astype(jnp.float32) for block in blocks], axis=1)
            for blocks in found
        )
        own_small = own_small.reshape(small_width).astype(jnp.float32)
    else:
        piece_width = small_width // copies
        out_rows = model_width // (shards * copies)
        packed = jnp.concatenate(
            [
                grad_out.astype(jnp.bfloat16).reshape(shards * copies, out_rows, model_width),
                jnp.pad(
                    small_grads.astype(jnp.bfloat16).reshape(shards * copies, 1, piece_width),
                    ((0, 0), (0, 7), (0, model_width - piece_width)),
                ),
            ],
            axis=1,
        )
        own_down = share(grad_down)
        own_up = share(grad_up)
        own_qkv = share(grad_qkv_w)
        own_packed = share(packed)
        own_out = own_packed[:, :out_rows].reshape(copies * out_rows, model_width)
        own_small = own_packed[:, out_rows, :piece_width].reshape(small_width)

    def own_part(start, width):
        return own_small[start : start + width]

    return (
        outputs,
        grad_inputs,
        own_qkv,
        own_out,
        own_up,
        own_down,
        own_part(0, 2 * part).reshape(2, part),
        own_part(2 * part, part),
        own_part(3 * part, hidden_part),
        own_part(rest, part),
        own_part(rest + part, part),
        own_part(rest + 2 * part, part),
        own_part(rest + 3 * part, part),
        own_part(rest + 4 * part, part),
    )


def solution(mesh):
    return jax.shard_map(
        body,
        mesh=mesh,
        in_specs=(
            P(("dp", "fsdp"), "ctx", None),
            P(("dp", "fsdp"), "ctx", None),
            P(),
            P("fsdp", None),
            P("fsdp", None),
            P("fsdp", None),
            P("fsdp", None),
            P(None, "fsdp"),
            P("fsdp"),
            P("fsdp"),
            P("fsdp"),
            P("fsdp"),
            P("fsdp"),
            P("fsdp"),
            P("fsdp"),
        ),
        out_specs=(
            P(("dp", "fsdp"), "ctx", None),
            P(("dp", "fsdp"), "ctx", None),
            P("fsdp", None),
            P("fsdp", None),
            P("fsdp", None),
            P("fsdp", None),
            P(None, "fsdp"),
            P("fsdp"),
            P("fsdp"),
            P("fsdp"),
            P("fsdp"),
            P("fsdp"),
            P("fsdp"),
            P("fsdp"),
        ),
        check_vma=False,
    )
```

```python
import math

import jax
import jax.numpy as jnp
from jax import lax
from jax.experimental import pallas as pl
from jax.experimental.pallas import tpu as pltpu
from jax.sharding import PartitionSpec as P

HEADS = 12
HD = 64


EPSILON = 1e-05
MASKED = -1e30
GELU_COEF = 0.7978845608028654


def gelu_tanh(pre_act):
    return (
        0.5
        * pre_act
        * (1.0 + jnp.tanh(GELU_COEF * (pre_act + 0.044715 * pre_act * pre_act * pre_act)))
    )


def normalize(rows_in):
    row_mean = jnp.mean(rows_in, axis=-1, keepdims=True)
    centered = rows_in - row_mean
    variance = jnp.mean(centered * centered, axis=-1, keepdims=True)
    row_scale = lax.rsqrt(variance + EPSILON)
    return (centered * row_scale, row_scale)


def norm_back(grad_out, normed, row_scale, gain_vec):
    shaped = grad_out * gain_vec
    return row_scale * (
        shaped
        - jnp.mean(shaped, axis=-1, keepdims=True)
        - normed * jnp.mean(shaped * normed, axis=-1, keepdims=True)
    )


def token_places(slot_ids, slot_order, piece_len):
    slot_block = slot_ids // piece_len
    block_ids = jnp.arange(slot_order.shape[0], dtype=jnp.int32)
    matches = (slot_block[:, None] == block_ids[None, :]).astype(jnp.int32)
    return jnp.sum(matches * slot_order[None, :], axis=1) * piece_len + slot_ids % piece_len


def attend_piece(state_now, piece_pair, queries, query_places, slot_order, piece_len, scaling):
    key_piece, value_piece = piece_pair
    seq_count = key_piece.shape[0]
    key_count = key_piece.shape[1]
    block_width = math.gcd(key_count, 512)
    block_count = key_count // block_width

    def one_block(block_index, carried):
        row_max, row_total, weighted = carried
        offset = block_index * block_width
        key_block = lax.dynamic_slice_in_dim(key_piece, offset, block_width, 1).reshape(
            seq_count, block_width, HEADS, HD
        )
        value_block = lax.dynamic_slice_in_dim(value_piece, offset, block_width, 1).reshape(
            seq_count, block_width, HEADS, HD
        )
        key_places = token_places(
            offset + jnp.arange(block_width, dtype=jnp.int32), slot_order, piece_len
        )
        scores = (
            jnp.einsum("sqhd,skhd->sqhk", queries, key_block, preferred_element_type=jnp.float32)
            * scaling
        )
        allowed = key_places[None, None, None, :] <= query_places[None, :, None, None]
        scores = jnp.where(allowed, scores, MASKED)
        new_max = jnp.maximum(row_max, jnp.max(scores, axis=-1))
        weights = jnp.where(allowed, jnp.exp(scores - new_max[..., None]), 0.0)
        factor = jnp.exp(row_max - new_max)
        row_total = row_total * factor + jnp.sum(weights, axis=-1)
        weighted = weighted * factor[..., None] + jnp.einsum(
            "sqhk,skhd->sqhd",
            weights.astype(jnp.bfloat16),
            value_block,
            preferred_element_type=jnp.float32,
        )
        return (new_max, row_total, weighted)

    return lax.fori_loop(0, block_count, one_block, state_now)


TILE = 16
MESH_ID = pl.DeviceIdType.MESH


def peer_table():
    dp, z, core = lax.axis_index("dp"), lax.axis_index("fsdp"), lax.axis_index("ctx")
    row, col = dp // 2, dp % 2
    sibling = {"ctx": 1 - core}
    beside = {"dp": row * 2 + (1 - col)}
    above = {"dp": (1 - row) * 2 + col}
    across = {"dp": (1 - row) * 2 + (1 - col)}
    return row, col, z, core, sibling, beside, above, across


def greet(peers):
    barrier = pltpu.get_barrier_semaphore()
    for peer in peers:
        pl.semaphore_signal(barrier, inc=1, device_id=peer, device_id_type=MESH_ID)
    pl.semaphore_wait(barrier, len(peers))


def push(source, target, sems, slot, peer):
    return pltpu.make_async_remote_copy(
        src_ref=source,
        dst_ref=target,
        send_sem=sems.at[0, slot],
        recv_sem=sems.at[1, slot],
        device_id=peer,
        device_id_type=MESH_ID,
    )


def half_of(ref, core):
    width = ref.shape[-1] // 2
    return pl.ds(pl.multiple_of(core * width, 128), width)


def gather_kernel(count, *refs):
    owns, wholes = refs[:count], refs[count : 2 * count]
    line_sems, plane_sems, pair_sems, keep_sems = refs[2 * count :]
    row, col, z, core, sibling, beside, above, across = peer_table()
    line_peers = [{"fsdp": lax.rem(z + 4 - k, 4)} for k in (1, 2, 3)]
    greet([sibling, beside, above, across] + line_peers)
    line = []
    for m, (own, whole) in enumerate(zip(owns, wholes)):
        half = half_of(own, core)
        for k in (0, 2, 1):
            line.append(
                push(
                    own.at[row, col, :, half],
                    whole.at[z, row, col, :, half],
                    line_sems,
                    m * 3 + k,
                    line_peers[k],
                )
            )
            line[-1].start()
    keeps = []
    for m, (own, whole) in enumerate(zip(owns, wholes)):
        keeps.append(pltpu.make_async_copy(own, whole.at[z], keep_sems.at[m]))
        keeps[-1].start()
    origins = [lax.rem(z + 1 + k, 4) for k in (0, 2, 1)]
    plane = []
    for m, whole in enumerate(wholes):
        half = half_of(whole, core)
        for step, origin in enumerate(origins):
            slot = m * 3 + step
            line[slot].wait_recv()
            piece = whole.at[origin, row, col, :, half]
            plane.append(
                [
                    push(piece, piece, plane_sems, slot * 3 + index, peer)
                    for index, peer in enumerate((beside, above, across))
                ]
            )
            for copy in plane[-1]:
                copy.start()
    pair = []
    for m, whole in enumerate(wholes):
        half = half_of(whole, core)
        for step, origin in enumerate(origins):
            slot = m * 3 + step
            for copy in plane[slot]:
                copy.wait_recv()
            piece = whole.at[origin, :, :, :, half]
            pair.append(push(piece, piece, pair_sems, slot, sibling))
            pair[-1].start()
    for copy in pair:
        copy.wait()
    for copies in plane:
        for copy in copies:
            copy.wait_send()
    for copy in line:
        copy.wait_send()
    for copy in keeps:
        copy.wait()


def gather_all(owns):
    count = len(owns)
    return pl.pallas_call(
        lambda *refs: gather_kernel(count, *refs),
        out_shape=tuple(jax.ShapeDtypeStruct((4,) + own.shape, own.dtype) for own in owns),
        in_specs=[pl.BlockSpec(memory_space=pl.ANY)] * count,
        out_specs=tuple([pl.BlockSpec(memory_space=pl.ANY)] * count),
        scratch_shapes=[
            pltpu.SemaphoreType.DMA((2, 3 * count)),
            pltpu.SemaphoreType.DMA((2, 9 * count)),
            pltpu.SemaphoreType.DMA((2, 3 * count)),
            pltpu.SemaphoreType.DMA((count,)),
        ],
        compiler_params=pltpu.CompilerParams(collective_id=1, has_side_effects=True),
        name="gather_weights",
    )(*owns)


def add_rows(pairs, start, rows):
    @pl.loop(0, 4)
    def _(shard):
        @pl.loop(0, rows // TILE)
        def _(step):
            offset = pl.multiple_of(step * TILE, TILE)
            for target, target_at, source, source_at in pairs:
                here = (shard,) + target_at + (pl.ds(start + offset, TILE),)
                there = (shard,) + source_at + (pl.ds(offset, TILE),)
                target[here] = (
                    target[here].astype(jnp.float32) + source[there].astype(jnp.float32)
                ).astype(target.dtype)


def first_cut(rows, width):
    return TILE if width >= 3072 else (rows // 2 + TILE - 1) // TILE * TILE


def sum_kernel(count, *refs):
    grads, shared = refs[:count], refs[count : 2 * count]
    groups = [refs[(2 + i) * count : (3 + i) * count] for i in range(7)]
    held, from_pair, from_beside, from_above, late_beside, late_above, from_line = groups
    (
        load_sems,
        pair_sems,
        beside_sems,
        above_sems,
        late_beside_sems,
        late_above_sems,
        line_sems,
        plane_sems,
        last_sems,
        own_sems,
    ) = refs[9 * count :]
    row, col, z, core, sibling, beside, above, across = peer_table()
    line_peers = [{"fsdp": lax.rem(z + 1 + k, 4)} for k in range(3)]
    greet([sibling, beside, above, across] + line_peers)
    loads, pairs = [], []
    for m in range(count):
        mine, theirs = half_of(grads[m], core), half_of(grads[m], 1 - core)
        pairs.append(
            push(grads[m].at[:, :, :, :, theirs], from_pair[m], pair_sems, m, sibling)
        )
        pairs[-1].start()
        loads.append(
            pltpu.make_async_copy(grads[m].at[:, :, :, :, mine], held[m], load_sems.at[m])
        )
        loads[-1].start()
    cuts = [first_cut(g.shape[3], g.shape[4]) for g in grads]
    tails = [g.shape[3] - cut for g, cut in zip(grads, cuts)]
    corners = [(r, c) for r in range(2) for c in range(2)]
    first = []
    for m in range(count):
        head, rest = pl.ds(0, cuts[m]), pl.ds(cuts[m], tails[m])
        loads[m].wait()
        pairs[m].wait_recv()
        add_rows([(held[m], at, from_pair[m], at) for at in corners], 0, cuts[m] + tails[m])
        first.append(
            (
                push(held[m].at[:, :, 1 - col, head], from_beside[m], beside_sems, m, beside),
                push(held[m].at[:, 1 - row, :, rest], from_above[m], above_sems, m, above),
            )
        )
        for copy in first[-1]:
            copy.start()
    second = []
    for m in range(count):
        head, rest = pl.ds(0, cuts[m]), pl.ds(cuts[m], tails[m])
        for copy in first[m]:
            copy.wait_recv()
        add_rows([(held[m], (r, col), from_beside[m], (r,)) for r in range(2)], 0, cuts[m])
        add_rows([(held[m], (row, c), from_above[m], (c,)) for c in range(2)], cuts[m], tails[m])
        second.append(
            (
                push(
                    held[m].at[:, 1 - row, col, head], late_above[m], late_above_sems, m, above
                ),
                push(
                    held[m].at[:, row, 1 - col, rest], late_beside[m], late_beside_sems, m, beside
                ),
            )
        )
        for copy in second[-1]:
            copy.start()
    line = []
    for m in range(count):
        for copy in second[m]:
            copy.wait_recv()
        add_rows([(held[m], (row, col), late_above[m], ())], 0, cuts[m])
        add_rows([(held[m], (row, col), late_beside[m], ())], cuts[m], tails[m])
        line.append(
            [
                push(
                    held[m].at[lax.rem(z + 1 + k, 4), row, col],
                    from_line[m].at[k],
                    line_sems,
                    m * 3 + k,
                    line_peers[k],
                )
                for k in range(3)
            ]
        )
        for copy in line[-1]:
            copy.start()
    plane, owns = [], []
    for m in range(count):
        for copy in line[m]:
            copy.wait_recv()

        @pl.loop(0, (cuts[m] + tails[m]) // TILE)
        def _(step):
            here = pl.ds(pl.multiple_of(step * TILE, TILE), TILE)
            total = held[m][z, row, col, here].astype(jnp.float32)
            for k in range(3):
                total = total + from_line[m][k, here].astype(jnp.float32)
            held[m][z, row, col, here] = total.astype(held[m].dtype)

        target = shared[m].at[row, col, :, half_of(shared[m], core)]
        plane.append(
            [
                push(held[m].at[z, row, col], target, plane_sems, m * 3 + index, peer)
                for index, peer in enumerate((beside, above, across))
            ]
        )
        for copy in plane[-1]:
            copy.start()
        owns.append(pltpu.make_async_copy(held[m].at[z, row, col], target, own_sems.at[m]))
        owns[-1].start()
    last = []
    for m in range(count):
        for copy in plane[m]:
            copy.wait_recv()
        owns[m].wait()
        piece = shared[m].at[:, :, :, half_of(shared[m], core)]
        last.append(push(piece, piece, last_sems, m, sibling))
        last[-1].start()
    for copies in first + second + line + plane:
        for copy in copies:
            copy.wait_send()
    for copy in pairs:
        copy.wait_send()
    for copy in last:
        copy.wait()


def sum_all(grads):
    count = len(grads)

    def rooms(shape_of):
        found = []
        for g in grads:
            rows, width = g.shape[-2:]
            cut = first_cut(rows, width)
            found.append(pltpu.VMEM(shape_of(rows, cut, rows - cut) + (width // 2,), g.dtype))
        return found

    return pl.pallas_call(
        lambda *refs: sum_kernel(count, *refs),
        out_shape=tuple(jax.ShapeDtypeStruct(g.shape[1:], g.dtype) for g in grads),
        in_specs=[pl.BlockSpec(memory_space=pl.ANY)] * count,
        out_specs=tuple([pl.BlockSpec(memory_space=pl.ANY)] * count),
        scratch_shapes=rooms(lambda rows, cut, tail: (4, 2, 2, rows))
        + rooms(lambda rows, cut, tail: (4, 2, 2, rows))
        + rooms(lambda rows, cut, tail: (4, 2, cut))
        + rooms(lambda rows, cut, tail: (4, 2, tail))
        + rooms(lambda rows, cut, tail: (4, tail))
        + rooms(lambda rows, cut, tail: (4, cut))
        + rooms(lambda rows, cut, tail: (3, rows))
        + [pltpu.SemaphoreType.DMA((count,))]
        + [pltpu.SemaphoreType.DMA((2, count))] * 5
        + [pltpu.SemaphoreType.DMA((2, 3 * count))] * 2
        + [pltpu.SemaphoreType.DMA((2, count)), pltpu.SemaphoreType.DMA((count,))],
        compiler_params=pltpu.CompilerParams(
            collective_id=2, has_side_effects=True, vmem_limit_bytes=48 * 1024 * 1024
        ),
        name="sum_gradients",
    )(*grads)


def body(
    inputs,
    cotangent,
    slot_order,
    w_qkv,
    w_out,
    w_up,
    w_down,
    qv_bias,
    out_bias,
    up_bias,
    down_bias,
    norm1_gain,
    norm1_shift,
    norm2_gain,
    norm2_shift,
):
    seq_count, local_len, model_width = inputs.shape
    row_count = seq_count * local_len
    piece_len = local_len // 2
    scaling = HD ** (-0.5)
    spread = ("fsdp", "dp", "ctx")
    copies = lax.axis_size("dp") * lax.axis_size("ctx")
    copy_index = lax.axis_index("dp") * lax.axis_size("ctx") + lax.axis_index("ctx")

    def own_piece(shard):
        rows = shard.shape[0] // copies
        return lax.dynamic_slice_in_dim(shard, copy_index * rows, rows, 0)

    def gather_whole(shard):
        return lax.all_gather(own_piece(shard), spread, axis=0, tiled=True)

    shards = lax.axis_size("fsdp")
    small_row = jnp.concatenate(
        [
            qv_bias.reshape(-1),
            out_bias,
            up_bias,
            down_bias,
            norm1_gain,
            norm1_shift,
            norm2_gain,
            norm2_shift,
        ]
    )
    part = model_width // shards
    fits = (lax.axis_size("dp"), shards, lax.axis_size("ctx")) == (4, 4, 2)
    small_lines = small_row.shape[0] // model_width

    def cut_rows(matrix, groups):
        return matrix.reshape(groups, 2, 2, -1, matrix.shape[-1])

    def with_small(matrix, small, groups):
        lines = small.reshape(groups, 1, 1, small_lines, model_width)
        lines = jnp.pad(lines, ((0, 0), (0, 1), (0, 1), (0, TILE - small_lines), (0, 0)))
        return jnp.concatenate([cut_rows(matrix, groups), lines], axis=3)

    def split_small(joined):
        rows = joined.shape[-2] - TILE
        matrix = joined[..., :rows, :].reshape(-1, model_width)
        small = joined[..., 0, 0, rows : rows + small_lines, :]
        return matrix, small.reshape(joined.shape[:-4] + (-1,))

    if fits:
        whole_qkv, joined, whole_up, whole_down = gather_all(
            (
                cut_rows(w_qkv, 1)[0],
                with_small(w_out, small_row, 1)[0],
                cut_rows(w_up, 1)[0],
                cut_rows(w_down, 1)[0],
            )
        )
        whole_out, small_rows = split_small(joined)
        whole_qkv, whole_up, whole_down = (
            whole.reshape(-1, whole.shape[-1]) for whole in (whole_qkv, whole_up, whole_down)
        )
    else:
        small_rows = lax.all_gather(small_row, "fsdp", axis=0, tiled=False)
        whole_qkv = gather_whole(w_qkv)
        whole_out = gather_whole(w_out)
        whole_up = gather_whole(w_up)
        whole_down = gather_whole(w_down)

    def small_part(start, width):
        return small_rows[:, start : start + width].reshape(-1)

    whole_qv = jnp.stack([small_part(0, part), small_part(part, part)])
    whole_ob = small_part(2 * part, part)
    hidden_part = up_bias.shape[0]
    whole_ub = small_part(3 * part, hidden_part)
    rest = 3 * part + hidden_part
    whole_db = small_part(rest, part)
    gain_one = small_part(rest + part, part)
    shift_one = small_part(rest + 2 * part, part)
    gain_two = small_part(rest + 3 * part, part)
    shift_two = small_part(rest + 4 * part, part)
    flat_in = inputs.reshape(row_count, model_width).astype(jnp.float32)
    normed_one, scale_one = normalize(flat_in)
    hidden_one = (normed_one * gain_one.astype(jnp.float32) + shift_one.astype(jnp.float32)).astype(
        jnp.bfloat16
    )
    projected = jnp.dot(hidden_one, whole_qkv, preferred_element_type=jnp.float32)
    bias_rows = whole_qv.astype(jnp.float32)
    queries = (
        (projected[:, :model_width] + bias_rows[0])
        .astype(jnp.bfloat16)
        .reshape(seq_count, local_len, HEADS, HD)
    )
    key_rows = (
        projected[:, model_width : 2 * model_width]
        .astype(jnp.bfloat16)
        .reshape(seq_count, local_len, model_width)
    )
    value_rows = (
        (projected[:, 2 * model_width :] + bias_rows[1])
        .astype(jnp.bfloat16)
        .reshape(seq_count, local_len, model_width)
    )
    slot_ids = lax.axis_index("ctx") * local_len + jnp.arange(local_len, dtype=jnp.int32)
    query_places = token_places(slot_ids, slot_order, piece_len)
    start_state = (
        jnp.full((seq_count, local_len, HEADS), MASKED, jnp.float32),
        jnp.zeros((seq_count, local_len, HEADS), jnp.float32),
        jnp.zeros((seq_count, local_len, HEADS, HD), jnp.float32),
    )
    final_state = attend_piece(
        start_state,
        (
            lax.all_gather(key_rows, "ctx", axis=1, tiled=True),
            lax.all_gather(value_rows, "ctx", axis=1, tiled=True),
        ),
        queries,
        query_places,
        slot_order,
        piece_len,
        scaling,
    )
    row_max, row_total, weighted = final_state
    attended_f32 = weighted / row_total[..., None]
    log_total = row_max + jnp.log(row_total)
    attended = attended_f32.reshape(row_count, model_width).astype(jnp.bfloat16)
    middle = (
        flat_in
        + jnp.dot(attended, whole_out, preferred_element_type=jnp.float32)
        + whole_ob.astype(jnp.float32)
    )
    normed_two, scale_two = normalize(middle)
    hidden_two = (normed_two * gain_two.astype(jnp.float32) + shift_two.astype(jnp.float32)).astype(
        jnp.bfloat16
    )
    pre_act = jnp.dot(hidden_two, whole_up, preferred_element_type=jnp.float32) + whole_ub.astype(
        jnp.float32
    )
    activated = gelu_tanh(pre_act).astype(jnp.bfloat16)
    result = (
        middle
        + jnp.dot(activated, whole_down, preferred_element_type=jnp.float32)
        + whole_db.astype(jnp.float32)
    )
    outputs = result.astype(jnp.bfloat16).reshape(seq_count, local_len, model_width)
    grad_rows = cotangent.reshape(row_count, model_width)
    grad_rows_f32 = grad_rows.astype(jnp.float32)
    grad_down = jnp.einsum("rf,rd->fd", activated, grad_rows, preferred_element_type=jnp.float32)
    grad_down_bias = jnp.sum(grad_rows_f32, axis=0)
    grad_act = jnp.einsum("rd,fd->rf", grad_rows, whole_down, preferred_element_type=jnp.float32)
    gelu_value, gelu_pull = jax.vjp(gelu_tanh, pre_act)
    grad_pre = gelu_pull(grad_act)[0].astype(jnp.bfloat16)
    grad_up = jnp.einsum("rd,rf->df", hidden_two, grad_pre, preferred_element_type=jnp.float32)
    grad_up_bias = jnp.sum(grad_pre.astype(jnp.float32), axis=0)
    grad_hidden_two = jnp.einsum(
        "rf,df->rd", grad_pre, whole_up, preferred_element_type=jnp.float32
    )
    grad_gain_two = jnp.sum(grad_hidden_two * normed_two, axis=0)
    grad_shift_two = jnp.sum(grad_hidden_two, axis=0)
    grad_middle = grad_rows_f32 + norm_back(
        grad_hidden_two, normed_two, scale_two, gain_two.astype(jnp.float32)
    )
    grad_branch = grad_middle.astype(jnp.bfloat16)
    grad_out = jnp.einsum("rd,re->de", attended, grad_branch, preferred_element_type=jnp.float32)
    grad_out_bias = jnp.sum(grad_branch.astype(jnp.float32), axis=0)
    grad_attended = (
        jnp.einsum("re,de->rd", grad_branch, whole_out, preferred_element_type=jnp.float32)
        .astype(jnp.bfloat16)
        .reshape(seq_count, local_len, HEADS, HD)
    )
    row_delta = jnp.sum(grad_attended.astype(jnp.float32) * attended_f32, axis=-1)
    gathered = (
        lax.all_gather(key_rows, "ctx", axis=1, tiled=True),
        lax.all_gather(value_rows, "ctx", axis=1, tiled=True),
    )
    gathered_keys, gathered_values = gathered
    key_count = gathered_keys.shape[1]
    block_width = math.gcd(local_len, 512)
    block_count = key_count // block_width

    def score_grads(
        query_block,
        grad_block,
        total_block,
        delta_block,
        block_places,
        key_block,
        value_block,
        key_places,
    ):
        allowed = key_places[None, None, None, :] <= block_places[None, :, None, None]
        scores = (
            jnp.einsum(
                "sqhd,skhd->sqhk", query_block, key_block, preferred_element_type=jnp.float32
            )
            * scaling
        )
        soft_probs = jnp.where(
            allowed, jnp.exp(jnp.where(allowed, scores - total_block[..., None], 0.0)), 0.0
        )
        grad_probs = jnp.einsum(
            "sqhd,skhd->sqhk", grad_block, value_block, preferred_element_type=jnp.float32
        )
        grad_scores = (soft_probs * (grad_probs - delta_block[..., None])).astype(jnp.bfloat16)
        return (soft_probs, grad_scores)

    def remote_block(offset):
        key_block = lax.dynamic_slice_in_dim(gathered_keys, offset, block_width, 1).reshape(
            seq_count, block_width, HEADS, HD
        )
        value_block = lax.dynamic_slice_in_dim(gathered_values, offset, block_width, 1).reshape(
            seq_count, block_width, HEADS, HD
        )
        key_places = token_places(
            offset + jnp.arange(block_width, dtype=jnp.int32), slot_order, piece_len
        )
        soft_probs, grad_scores = score_grads(
            queries,
            grad_attended,
            log_total,
            row_delta,
            query_places,
            key_block,
            value_block,
            key_places,
        )
        return (key_block, soft_probs, grad_scores)

    zero_queries = jnp.zeros((seq_count, local_len, HEADS, HD), jnp.float32)

    def back_block(grad_queries, block_index):
        key_block, soft_probs, grad_scores = remote_block(block_index * block_width)
        grad_queries = (
            grad_queries
            + jnp.einsum(
                "sqhk,skhd->sqhd", grad_scores, key_block, preferred_element_type=jnp.float32
            )
            * scaling
        )
        grad_keys = (
            jnp.einsum("sqhk,sqhd->skhd", grad_scores, queries, preferred_element_type=jnp.float32)
            * scaling
        )
        grad_values = jnp.einsum(
            "sqhk,sqhd->skhd",
            soft_probs.astype(jnp.bfloat16),
            grad_attended,
            preferred_element_type=jnp.float32,
        )
        key_term = jnp.concatenate(
            [
                grad_keys.reshape(seq_count, block_width, model_width),
                grad_values.reshape(seq_count, block_width, model_width),
            ],
            axis=-1,
        )
        return (grad_queries, key_term)

    grad_queries, key_terms = lax.scan(
        back_block, zero_queries, jnp.arange(block_count, dtype=jnp.int32)
    )
    own_terms = lax.psum_scatter(
        key_terms.astype(jnp.bfloat16), "ctx", scatter_dimension=0, tiled=True
    ).astype(jnp.float32)
    own_terms = own_terms.transpose(1, 0, 2, 3).reshape(row_count, 2 * model_width)
    grad_qkv = jnp.concatenate(
        [grad_queries.reshape(row_count, model_width), own_terms], axis=-1
    ).astype(jnp.bfloat16)
    grad_qkv_w = jnp.einsum("rd,re->de", hidden_one, grad_qkv, preferred_element_type=jnp.float32)
    column_sums = jnp.sum(grad_qkv.astype(jnp.float32), axis=0)
    grad_qv_bias = jnp.stack([column_sums[:model_width], column_sums[2 * model_width :]])
    grad_hidden_one = jnp.einsum(
        "re,de->rd", grad_qkv, whole_qkv, preferred_element_type=jnp.float32
    )
    grad_gain_one = jnp.sum(grad_hidden_one * normed_one, axis=0)
    grad_shift_one = jnp.sum(grad_hidden_one, axis=0)
    grad_inputs = (
        (
            grad_middle
            + norm_back(grad_hidden_one, normed_one, scale_one, gain_one.astype(jnp.float32))
        )
        .astype(jnp.bfloat16)
        .reshape(seq_count, local_len, model_width)
    )
    def share(grad):
        piece = lax.psum_scatter(
            grad.astype(jnp.bfloat16), spread, scatter_dimension=0, tiled=True
        )
        return lax.all_gather(piece, ("dp", "ctx"), axis=0, tiled=True).astype(jnp.float32)

    small_grads = jnp.concatenate(
        [
            grad_qv_bias[0].reshape(shards, part),
            grad_qv_bias[1].reshape(shards, part),
            grad_out_bias.reshape(shards, part),
            grad_up_bias.reshape(shards, hidden_part),
            grad_down_bias.reshape(shards, part),
            grad_gain_one.reshape(shards, part),
            grad_shift_one.reshape(shards, part),
            grad_gain_two.reshape(shards, part),
            grad_shift_two.reshape(shards, part),
        ],
        axis=1,
    )
    small_width = small_grads.shape[1]
    if fits:
        up_sum, down_sum, qkv_sum, joined = sum_all(
            (
                cut_rows(grad_up.astype(jnp.bfloat16), shards),
                cut_rows(grad_down.astype(jnp.bfloat16), shards),
                cut_rows(grad_qkv_w.astype(jnp.bfloat16), shards),
                with_small(
                    grad_out.astype(jnp.bfloat16), small_grads.astype(jnp.bfloat16), shards
                ),
            )
        )
        own_qkv, own_up, own_down = (
            g.reshape(-1, g.shape[-1]).astype(jnp.float32) for g in (qkv_sum, up_sum, down_sum)
        )
        own_out, own_small = (g.astype(jnp.float32) for g in split_small(joined))
    else:
        piece_width = small_width // copies
        out_rows = model_width // (shards * copies)
        packed = jnp.concatenate(
            [
                grad_out.astype(jnp.bfloat16).reshape(shards * copies, out_rows, model_width),
                jnp.pad(
                    small_grads.astype(jnp.bfloat16).reshape(shards * copies, 1, piece_width),
                    ((0, 0), (0, 7), (0, model_width - piece_width)),
                ),
            ],
            axis=1,
        )
        own_down = share(grad_down)
        own_up = share(grad_up)
        own_qkv = share(grad_qkv_w)
        own_packed = share(packed)
        own_out = own_packed[:, :out_rows].reshape(copies * out_rows, model_width)
        own_small = own_packed[:, out_rows, :piece_width].reshape(small_width)

    def own_part(start, width):
        return own_small[start : start + width]

    return (
        outputs,
        grad_inputs,
        own_qkv,
        own_out,
        own_up,
        own_down,
        own_part(0, 2 * part).reshape(2, part),
        own_part(2 * part, part),
        own_part(3 * part, hidden_part),
        own_part(rest, part),
        own_part(rest + part, part),
        own_part(rest + 2 * part, part),
        own_part(rest + 3 * part, part),
        own_part(rest + 4 * part, part),
    )


def solution(mesh):
    return jax.shard_map(
        body,
        mesh=mesh,
        in_specs=(
            P(("dp", "fsdp"), "ctx", None),
            P(("dp", "fsdp"), "ctx", None),
            P(),
            P("fsdp", None),
            P("fsdp", None),
            P("fsdp", None),
            P("fsdp", None),
            P(None, "fsdp"),
            P("fsdp"),
            P("fsdp"),
            P("fsdp"),
            P("fsdp"),
            P("fsdp"),
            P("fsdp"),
            P("fsdp"),
        ),
        out_specs=(
            P(("dp", "fsdp"), "ctx", None),
            P(("dp", "fsdp"), "ctx", None),
            P("fsdp", None),
            P("fsdp", None),
            P("fsdp", None),
            P("fsdp", None),
            P(None, "fsdp"),
            P("fsdp"),
            P("fsdp"),
            P("fsdp"),
            P("fsdp"),
            P("fsdp"),
            P("fsdp"),
            P("fsdp"),
        ),
        check_vma=False,
    )
```
